256 devices in a mesh: var: 16 (over z, core), layer: 16 (over y, x).
Axes of the slice: x: 4, y: 4, z: 8, core: 2. Of those that a mesh axis runs over, the one named last changes fastest.
Arguments:
- sample_matrix: bfloat16 [1024, 65536], P('layer', 'var'), may hold values from -6 to 6
- precision_blocks: float32 [256, 256, 4, 256], P('layer', 'var'), may hold values from -1 to 2, as said below
- block_pattern: int32 [256, 4], P('var'), may hold values from 0 to 255, as said below
- block_counts: int32 [256], P('var'), may hold values from 1 to 4
- candidate_cols: int32 [256, 6], P('var'), may hold values from 0 to 255, as said below
Outputs:
- updated_blocks: float32 [256, 256, 6, 256], P('layer', 'var')
The draws below stay inside these ranges and needn't reach their ends.
Inputs may be any that keep to these rules, and one draw needn't show every extreme that they name: `block_pattern`: slot 0 of block row i is i; the 4 entries of a row are distinct. `candidate_cols`: slot 0 of block row i is i; the 6 entries of a row are distinct and include every entry of that row of block_pattern. `precision_blocks`: entry (r, r) of slot 0 of every block row lies in 0.5 to 2.
All inputs are finite; a program needn't handle non-finite values.
Results may differ from the reference program's by a relative error of at most 0.014.
Values may be sent and summed in bfloat16 or wider, within the bound.
A program may use at most 128 MiB of HBM per device.

```python
import math
import jax
import jax.numpy as jnp
from jax import lax

BLOCK = 256
SAMPLES_DEV = 64
STORED = 4
CANDIDATES = 6
NBLOCKS = 256
VARIABLES = 65536
SAMPLES = 1024
N_LAYER = 16


def block_offsets(key):
    scores = jax.random.randint(key, (NBLOCKS, NBLOCKS - 1), 0, 2 ** 20) * NBLOCKS + jnp.arange(NBLOCKS - 1)[None, :]
    picked = lax.top_k(scores, CANDIDATES - 1)[1] + 1
    return (jnp.arange(NBLOCKS)[:, None] + picked) % NBLOCKS


def draw_block_pattern(key, part):
    shared = block_offsets(key)
    rows = jnp.arange(NBLOCKS)[:, None]
    return jnp.concatenate([rows, shared[:, :STORED - 1]], axis=1).astype(jnp.int32)


def draw_candidate_cols(key, part):
    shared = block_offsets(key)
    rows = jnp.arange(NBLOCKS)[:, None]
    return jnp.concatenate([rows, shared[:, ::-1]], axis=1).astype(jnp.int32)


def draw_precision_blocks(key, part):
    key = jax.random.fold_in(key, 11)
    first_key, second_key = jax.random.split(key)
    shape = (BLOCK, NBLOCKS, STORED, BLOCK)
    spread = 0.03 * jax.random.normal(first_key, shape, jnp.float32)
    diagonal = jnp.exp(jax.random.uniform(second_key, (BLOCK, NBLOCKS), jnp.float32, math.log(0.5), math.log(2.0)))
    row_ids = jnp.arange(BLOCK)[:, None, None, None]
    col_ids = jnp.arange(BLOCK)[None, None, None, :]
    slot_ids = jnp.arange(STORED)[None, None, :, None]
    on_diag = (row_ids == col_ids) & (slot_ids == 0)
    return jnp.where(on_diag, diagonal[:, :, None, None], spread).astype(jnp.float32)


def plant(result, key, low, largest):
    extent = result.shape
    index_at = [jax.random.randint(jax.random.fold_in(key, axis), (), 0, extent[axis]) for axis in range(len(extent))]
    result = result.at[tuple(index_at)].set(low)
    longest = extent.index(max(extent))
    index_at[longest] = (index_at[longest] + 1) % extent[longest]
    return result.at[tuple(index_at)].set(largest)


def steps_of(stream_key, extent, shards, low, high):
    gain, own = 1.0, jax.random.fold_in(stream_key, 6)
    for dim, parts in shards:
        heights = jnp.exp(jax.random.uniform(jax.random.fold_in(own, dim), (parts,), jnp.float32, low / len(shards), high / len(shards)))
        gain = gain * jnp.repeat(heights, extent[dim] // parts).reshape([-1 if axis == dim else 1 for axis in range(len(extent))])
    return gain


def noise(stream_key, shape, scale, bound, cuts=(), kind=jnp.bfloat16):
    result = scale * jax.random.normal(stream_key, shape, jnp.float32)
    if cuts:
        result = result * steps_of(stream_key, shape, cuts, -0.22, 0.18)
    return jnp.clip(result, -bound, bound).astype(kind)


def setup_inputs(seed: int = 0) -> dict:
    splits = jax.random.split(jax.random.key(seed), 6)
    sample_matrix = noise(splits[0], (SAMPLES, VARIABLES), 1.0, 6.0, ((0, 16), (1, 16)))
    precision_blocks = draw_precision_blocks(jax.random.fold_in(splits[5], 71), 0)
    block_pattern = draw_block_pattern(jax.random.fold_in(splits[5], 71), 0)
    block_counts = plant(jax.random.randint(splits[3], (NBLOCKS,), 1, STORED + 1), jax.random.fold_in(splits[3], 1), 1, STORED).astype(jnp.int32)
    candidate_cols = draw_candidate_cols(jax.random.fold_in(splits[5], 71), 0)
    return dict(sample_matrix=sample_matrix, precision_blocks=precision_blocks, block_pattern=block_pattern, block_counts=block_counts, candidate_cols=candidate_cols)


step_size = 0.5
penalty = 0.04


def reference(sample_matrix, precision_blocks, block_pattern, block_counts, candidate_cols):
    live_slots = jnp.arange(STORED)[None, :] < block_counts[:, None]
    half_blocks = jnp.where(live_slots[None, :, :, None], precision_blocks, 0.0).astype(jnp.bfloat16)
    column_blocks = sample_matrix.reshape(SAMPLES, NBLOCKS, BLOCK)

    def product_row(row_index):
        weights = half_blocks[:, row_index].astype(jnp.float32)
        needed = jnp.take(column_blocks, block_pattern[row_index], axis=1).astype(jnp.float32)
        return jnp.einsum("rkc,skc->sr", weights, needed).astype(jnp.bfloat16)

    products = lax.map(product_row, jnp.arange(NBLOCKS))
    eye_mask = jnp.arange(BLOCK)[:, None] == jnp.arange(BLOCK)[None, :]
    first_slot = (jnp.arange(CANDIDATES) == 0)[:, None, None]
    diag_mask = first_slot & eye_mask[None]

    def update_row(row_index):
        own_columns = column_blocks[:, row_index].astype(jnp.float32).reshape(N_LAYER, SAMPLES_DEV, BLOCK)
        own_products = products[row_index].astype(jnp.float32).reshape(N_LAYER, SAMPLES_DEV, BLOCK)
        chosen = candidate_cols[row_index]
        far_columns = jnp.take(column_blocks, chosen, axis=1).astype(jnp.float32).reshape(N_LAYER, SAMPLES_DEV, CANDIDATES, BLOCK)
        far_products = jnp.take(products, chosen, axis=0).astype(jnp.float32).reshape(CANDIDATES, N_LAYER, SAMPLES_DEV, BLOCK)
        layer_terms = jnp.einsum("gsr,cgsq->gcrq", own_columns, far_products) + jnp.einsum("gsr,gscq->gcrq", own_products, far_columns)
        rounded = lax.optimization_barrier(layer_terms.astype(jnp.bfloat16)).astype(jnp.float32)
        gradient = jnp.sum(rounded, axis=0) / (2.0 * SAMPLES)
        own_blocks = precision_blocks[:, row_index]
        diagonal = jnp.sum(jnp.where(eye_mask, own_blocks[:, 0, :], 0.0), axis=1)
        gradient = gradient - jnp.where(diag_mask, (1.0 / diagonal)[None, :, None], 0.0)
        matches = (chosen[:, None] == block_pattern[row_index][None, :]) & live_slots[row_index][None, :]
        previous = jnp.sum(jnp.where(matches[:, :, None, None], jnp.transpose(own_blocks, (1, 0, 2))[None], 0.0), axis=1)
        stepped = previous - step_size * gradient
        shrunk = jnp.sign(stepped) * jnp.maximum(jnp.abs(stepped) - step_size * penalty, 0.0)
        return jnp.where(diag_mask, stepped, shrunk)

    updated = lax.map(update_row, jnp.arange(NBLOCKS))
    return jnp.transpose(updated, (2, 0, 1, 3))
```

```python
import jax
import jax.numpy as jnp
from jax import lax
from jax.experimental import pallas as pl
from jax.experimental.pallas import tpu as pltpu
from jax.sharding import PartitionSpec as P

step_size = 0.5
penalty = 0.04

NZ, NC, NY, NX = 8, 2, 4, 4
BLOCKS = 16
SAMP = 64
HALF = 128
SLOTS = 6
CHUNKS = 14
MESH = pl.DeviceIdType.MESH
bf16, f32 = jnp.bfloat16, jnp.float32

PARTS = (("x", 1), ("x", -1), ("y", 1), ("y", -1))


def kernel(x_ref, w_ref, pat_ref, cand_ref, out_ref,
           xg, pg0, pg1, wg, at, terms, fwd1, part, fwd2, m1, m23, n1, n23,
           x_rs, x_ss, xp_rs, xp_ss, w_rs, w_ss, p_rs, p_ss, pp_rs, pp_ss,
           m1_rs, m23_rs, n1_rs, n23_rs, t_ss, r_ss, own_sem):
    v = lax.axis_index("var")
    l = lax.axis_index("layer")
    z, core = v // NC, v % NC
    y, x = l // NX, l % NX
    here = {"x": x, "y": y}
    size = {"x": NX, "y": NY}

    def at_z(step):
        return {"var": ((z + step + NZ) % NZ) * NC + core, "layer": l}

    def at_xy(axis, step):
        if axis == "x":
            return {"var": v, "layer": y * NX + (x + step + NX) % NX}
        return {"var": v, "layer": ((y + step + NY) % NY) * NX + x}

    partner = {"var": z * NC + (1 - core), "layer": l}

    barrier = pltpu.get_barrier_semaphore()
    greeted = [at_z(1), at_z(-1), partner, at_xy("x", 1), at_xy("x", -1), at_xy("y", 1), at_xy("y", -1)]
    for device in greeted:
        pl.semaphore_signal(barrier, inc=1, device_id=device, device_id_type=MESH)

    for j in range(BLOCKS):
        for h in range(2):
            start = (j * 2 + h) * HALF
            xg[v * BLOCKS + j, h] = x_ref[:, start:start + HALF]
    own_w = pltpu.make_async_copy(w_ref, wg.at[l], own_sem)
    own_w.start()
    pl.semaphore_wait(barrier, len(greeted))

    def push(src, dst, ss, rs, device):
        pltpu.make_async_remote_copy(src_ref=src, dst_ref=dst, send_sem=ss, recv_sem=rs,
                                     device_id=device, device_id_type=MESH).start()

    def arrived(ref, sem):
        pltpu.make_async_copy(ref, ref, sem).wait()

    def x_piece(vsrc, p):
        return xg.at[pl.ds(vsrc * BLOCKS + p * 4, 4)]

    def x_ring(vsrc, p, sign, hop):
        ref = x_piece(vsrc, p)
        push(ref, ref, x_ss, x_rs.at[0 if sign > 0 else 1, hop - 1, p], at_z(sign))

    def x_hop(h):
        for p in range(4):
            for sign in (1, -1):
                last = 4 if (p < 2) == (sign > 0) else 3
                if h > last:
                    continue
                vsrc = ((z - sign * h + NZ) % NZ) * NC + core
                ref = x_piece(vsrc, p)
                arrived(ref, x_rs.at[0 if sign > 0 else 1, h - 1, p])
                if h < last:
                    x_ring(vsrc, p, sign, h + 1)
                push(ref, ref, xp_ss, xp_rs, partner)

    for p in range(4):
        for sign in (1, -1):
            x_ring(v, p, sign, 1)

    def w_piece(lsrc, q):
        return wg.at[lsrc, q]

    def w_send(lsrc, q, axis, step):
        ref = w_piece(lsrc, q)
        push(ref, ref, w_ss, w_rs.at[q, lsrc], at_xy(axis, step))

    def w_wait(lsrc, q):
        arrived(w_piece(lsrc, q), w_rs.at[q, lsrc])

    def other(axis):
        return "y" if axis == "x" else "x"

    def l_at(first, a, second, b):
        pos = dict(here)
        pos[first] = (pos[first] + a + 4) % 4
        pos[second] = (pos[second] + b + 4) % 4
        return pos["y"] * NX + pos["x"]

    def each():
        for q, (d1, s) in enumerate(PARTS):
            yield q, d1, other(d1), s

    own_w.wait()
    for q, d1, d2, s in each():
        for step in (1, -1):
            w_send(l, q, d1, step)
    for q, d1, d2, s in each():
        for step in (1, -1):
            w_send(l, q, d2, step)
    push(xg.at[pl.ds(v * BLOCKS, BLOCKS)], xg.at[pl.ds(v * BLOCKS, BLOCKS)], xp_ss, xp_rs, partner)

    for q, d1, d2, s in each():
        for a in (-s, s):
            lsrc = l_at(d1, a, d2, 0)
            w_wait(lsrc, q)
            if a == -s:
                w_send(lsrc, q, d1, s)
            for step in (1, -1):
                w_send(lsrc, q, d2, step)
    x_hop(1)
    for q, d1, d2, s in each():
        for b in (-s, s):
            lsrc = l_at(d1, 0, d2, b)
            w_wait(lsrc, q)
            if b == -s:
                w_send(lsrc, q, d2, s)
    for q, d1, d2, s in each():
        lsrc = l_at(d1, 2, d2, 0)
        w_wait(lsrc, q)
        for step in (1, -1):
            w_send(lsrc, q, d2, step)
    x_hop(2)
    for a in (-1, 1, 2):
        for q, d1, d2, s in each():
            for b in (-s, s):
                lsrc = l_at(d1, a, d2, b)
                w_wait(lsrc, q)
                if b == -s:
                    w_send(lsrc, q, d2, s)
        if a == 1:
            x_hop(3)
    x_hop(4)
    arrived(xg.at[pl.ds(0, NZ * BLOCKS)], xp_rs)
    for a in (0, -1, 1, 2):
        for q, d1, d2, s in each():
            w_wait(l_at(d1, a, d2, 2), q)

    def product(i, carry):
        total = jnp.zeros((SAMP, 2 * HALF), f32)
        for k in range(4):
            j = pat_ref[i, k]
            cols = jnp.concatenate([xg[j, 0], xg[j, 1]], axis=1)
            rows = wg[:, i // 4, i % 4, k].reshape(2 * HALF, 2 * HALF)
            total += lax.dot_general(cols, rows, (((1,), (1,)), ((), ())), preferred_element_type=f32)
        result = total.astype(bf16)
        pg0[v * BLOCKS + i] = result[:, :HALF]
        pg1[v * BLOCKS + i] = result[:, HALF:]
        own = jnp.concatenate([xg[v * BLOCKS + i, 0], xg[v * BLOCKS + i, 1]], axis=1)
        both = jnp.concatenate([own.astype(f32), result.astype(f32)], axis=0)
        at[i] = both.T.astype(bf16)
        return carry

    lax.fori_loop(0, BLOCKS, product, 0)

    def p_piece(pg, vsrc, p):
        return pg.at[pl.ds(vsrc * BLOCKS + p * 8, 8)]

    def p_ring(qh, pg, vsrc, p, sign, hop):
        ref = p_piece(pg, vsrc, p)
        push(ref, ref, p_ss.at[qh], p_rs.at[qh, 0 if sign > 0 else 1, hop - 1, p], at_z(sign))

    def p_start(qh, pg):
        for p in range(2):
            for sign in (1, -1):
                p_ring(qh, pg, v, p, sign, 1)
        ref = pg.at[pl.ds(v * BLOCKS, BLOCKS)]
        push(ref, ref, pp_ss.at[qh], pp_rs.at[qh], partner)

    def p_hop(qh, pg, h):
        for p in range(2):
            for sign in (1, -1):
                last = 4 if (p == 0) == (sign > 0) else 3

                def step(p=p, sign=sign, last=last):
                    vsrc = ((z - sign * h + NZ) % NZ) * NC + core
                    ref = p_piece(pg, vsrc, p)
                    arrived(ref, p_rs.at[qh, 0 if sign > 0 else 1, h - 1, p])

                    @pl.when(h < last)
                    def _():
                        p_ring(qh, pg, vsrc, p, sign, h + 1)
                    push(ref, ref, pp_ss.at[qh], pp_rs.at[qh], partner)

                if last == 4:
                    step()
                else:
                    pl.when(h <= 3)(step)

        @pl.when(h == 4)
        def _():
            arrived(pg.at[pl.ds(0, NZ * BLOCKS)], pp_rs.at[qh])

    def place(axis, step):
        return (here[axis] + step + 4) % 4

    def stage0(u, qh, pg, own):
        slot = u % SLOTS
        for q, d1, d2, s in each():
            def one(i4, carry, q=q, d1=d1):
                i = q * 4 + i4
                if own:
                    j = v * BLOCKS + i
                else:
                    j = cand_ref[i, u - (3 if qh == 0 else 8)]
                right = jnp.concatenate([pg[j], xg[j, qh]], axis=0)
                term = jnp.dot(at[i], right, preferred_element_type=f32).astype(bf16)
                for a in range(4):
                    for b in range(4):
                        row = 16 * ((b * NX + a) if d1 == "x" else (a * NX + b))
                        terms[slot, q, a, b, i4] = term[row:row + 16]
                return carry

            for i4 in range(4):
                one(i4, 0)
            push(terms.at[slot, q, place(d1, 2)], m1.at[u, q], t_ss.at[slot], m1_rs.at[u], at_xy(d1, s))
            push(terms.at[slot, q, place(d1, -s)], m23.at[u, q, 0], t_ss.at[slot], m23_rs.at[u], at_xy(d1, -s))

    def stage1(u):
        slot = u % SLOTS
        arrived(m1.at[u], m1_rs.at[u])
        for q, d1, d2, s in each():
            fwd1[slot, q] = (terms[slot, q, place(d1, s)].astype(f32) + m1[u, q].astype(f32)).astype(bf16)
            push(fwd1.at[slot, q], m23.at[u, q, 1], t_ss.at[slot], m23_rs.at[u], at_xy(d1, s))

    def stage2(u):
        slot = u % SLOTS
        arrived(m23.at[u], m23_rs.at[u])
        for q, d1, d2, s in each():
            part[slot, q] = (terms[slot, q, place(d1, 0)].astype(f32) + m23[u, q, 0].astype(f32)
                             + m23[u, q, 1].astype(f32)).astype(bf16)
            push(part.at[slot, q, place(d2, 2)], n1.at[u, q], r_ss.at[slot], n1_rs.at[u], at_xy(d2, s))
            push(part.at[slot, q, place(d2, -s)], n23.at[u, q, 0], r_ss.at[slot], n23_rs.at[u], at_xy(d2, -s))

    def stage3(u):
        slot = u % SLOTS
        arrived(n1.at[u], n1_rs.at[u])
        for q, d1, d2, s in each():
            fwd2[slot, q] = (part[slot, q, place(d2, s)].astype(f32) + n1[u, q].astype(f32)).astype(bf16)
            push(fwd2.at[slot, q], n23.at[u, q, 1], r_ss.at[slot], n23_rs.at[u], at_xy(d2, s))

    def stage4(u):
        slot = u % SLOTS
        arrived(n23.at[u], n23_rs.at[u])
        for q, d1, d2, s in each():
            out_ref[u, pl.ds(q * 4, 4)] = (part[slot, q, place(d2, 0)].astype(f32) + n23[u, q, 0].astype(f32)
                                           + n23[u, q, 1].astype(f32))
        arrived(terms.at[slot, pl.ds(0, 3)], t_ss.at[slot])
        arrived(part.at[slot, pl.ds(0, 3)], r_ss.at[slot])

    def filled(u):
        return ((u >= 0) & (u < 2)) | ((u >= 4) & (u < CHUNKS))

    p_start(0, pg0)

    def turn(u, carry):
        pl.when(u == 0)(lambda: stage0(u, 0, pg0, True))
        pl.when(u == 1)(lambda: stage0(u, 1, pg1, True))
        pl.when((u >= 4) & (u < 9))(lambda: stage0(u, 0, pg0, False))
        pl.when((u >= 9) & (u < 14))(lambda: stage0(u, 1, pg1, False))
        pl.when(filled(u - 1))(lambda: stage1(u - 1))
        pl.when(filled(u - 2))(lambda: stage2(u - 2))
        pl.when(filled(u - 3))(lambda: stage3(u - 3))
        pl.when(filled(u - 4))(lambda: stage4(u - 4))
        pl.when(u < 4)(lambda: p_hop(0, pg0, u + 1))
        pl.when(u == 2)(lambda: p_start(1, pg1))
        pl.when((u >= 4) & (u < 8))(lambda: p_hop(1, pg1, u - 3))
        return carry

    lax.fori_loop(0, CHUNKS + 4, turn, 0)

    arrived(xg.at[pl.ds(0, 7 * BLOCKS)], x_ss)
    arrived(xg.at[pl.ds(0, 8 * BLOCKS)], xp_ss)
    arrived(wg.at[pl.ds(0, 15)], w_ss)
    for qh, pg in enumerate((pg0, pg1)):
        arrived(pg.at[pl.ds(0, 7 * BLOCKS)], p_ss.at[qh])
        arrived(pg.at[pl.ds(0, 8 * BLOCKS)], pp_ss.at[qh])


def step(sample_matrix, half, block_pattern, candidate_cols):
    vmem = pl.BlockSpec(memory_space=pltpu.VMEM)
    smem = pl.BlockSpec(memory_space=pltpu.SMEM)
    dma = pltpu.SemaphoreType.DMA
    scratch = [
        pltpu.VMEM((256, 2, SAMP, HALF), bf16),
        pltpu.VMEM((256, SAMP, HALF), bf16),
        pltpu.VMEM((256, SAMP, HALF), bf16),
        pltpu.VMEM((16, 4, 4, 4, 16, 256), bf16),
        pltpu.VMEM((BLOCKS, 256, 128), bf16),
        pltpu.VMEM((SLOTS, 4, 4, 4, 4, 16, HALF), bf16),
        pltpu.VMEM((SLOTS, 4, 4, 4, 16, HALF), bf16),
        pltpu.VMEM((SLOTS, 4, 4, 4, 16, HALF), bf16),
        pltpu.VMEM((SLOTS, 4, 4, 16, HALF), bf16),
        pltpu.VMEM((CHUNKS, 4, 4, 4, 16, HALF), bf16),
        pltpu.VMEM((CHUNKS, 4, 2, 4, 4, 16, HALF), bf16),
        pltpu.VMEM((CHUNKS, 4, 4, 16, HALF), bf16),
        pltpu.VMEM((CHUNKS, 4, 2, 4, 16, HALF), bf16),
        dma((2, 4, 4)), dma(()), dma(()), dma(()),
        dma((4, 16)), dma(()),
        dma((2, 2, 4, 2)), dma((2,)), dma((2,)), dma((2,)),
        dma((CHUNKS,)), dma((CHUNKS,)), dma((CHUNKS,)), dma((CHUNKS,)), dma((SLOTS,)), dma((SLOTS,)), dma(()),
    ]
    return pl.pallas_call(
        kernel,
        out_shape=jax.ShapeDtypeStruct((CHUNKS, BLOCKS, 16, HALF), f32),
        in_specs=[vmem, vmem, smem, smem],
        out_specs=vmem,
        scratch_shapes=scratch,
        compiler_params=pltpu.CompilerParams(
            collective_id=0, has_side_effects=True, vmem_limit_bytes=60 * 2 ** 20),
    )(sample_matrix, half, block_pattern, candidate_cols)


def body(sample_matrix, precision_blocks, block_pattern, block_counts, candidate_cols):
    layer_count = lax.axis_size("layer")
    layer_index = lax.axis_index("layer")
    rows_here, local_rows, stored, block_width = precision_blocks.shape
    per_layer = sample_matrix.shape[0]
    chosen_count = candidate_cols.shape[1]
    total_samples = per_layer * layer_count
    live_slots = jnp.arange(stored)[None, :] < block_counts[:, None]
    half_blocks = jnp.where(live_slots[None, :, :, None], precision_blocks, 0.0).astype(jnp.bfloat16)
    half = jnp.transpose(half_blocks, (1, 2, 0, 3)).reshape(4, 4, stored, rows_here, block_width)
    sums = step(sample_matrix, half, block_pattern, candidate_cols)
    first = jnp.transpose(sums[0:2], (2, 1, 0, 3)).reshape(rows_here, local_rows, 1, block_width)
    rest = jnp.transpose(sums[4:].reshape(2, 5, local_rows, rows_here, HALF), (3, 2, 1, 0, 4))
    rest = rest.reshape(rows_here, local_rows, 5, block_width)
    gradient = jnp.concatenate([first, rest], axis=2) / (2.0 * total_samples)
    global_rows = layer_index * rows_here + jnp.arange(rows_here)
    eye_mask = global_rows[:, None] == jnp.arange(block_width)[None, :]
    diagonal = jnp.sum(jnp.where(eye_mask[:, None, :], precision_blocks[:, :, 0, :], 0.0), axis=2)
    first_slot = jnp.arange(chosen_count) == 0
    diag_mask = eye_mask[:, None, None, :] & first_slot[None, None, :, None]
    gradient = gradient - jnp.where(diag_mask, (1.0 / diagonal)[:, :, None, None], 0.0)
    matches = (candidate_cols[:, :, None] == block_pattern[:, None, :]) & live_slots[:, None, :]
    previous = jnp.zeros(gradient.shape, jnp.float32)
    for slot_index in range(stored):
        previous = previous + jnp.where(
            matches[None, :, :, slot_index, None], precision_blocks[:, :, None, slot_index, :], 0.0
        )
    stepped = previous - step_size * gradient
    shrunk = jnp.sign(stepped) * jnp.maximum(jnp.abs(stepped) - step_size * penalty, 0.0)
    return jnp.where(diag_mask, stepped, shrunk)


def solution(mesh):
    placed = (
        P("layer", "var"),
        P("layer", "var", None, None),
        P("var", None),
        P("var"),
        P("var", None),
    )
    return jax.shard_map(
        body, mesh=mesh, in_specs=placed, out_specs=P("layer", "var", None, None), check_vma=False
    )
```

```python
import jax
import jax.numpy as jnp
from jax import lax
from jax.experimental import pallas as pl
from jax.experimental.pallas import tpu as pltpu
from jax.sharding import PartitionSpec as P

step_size = 0.5
penalty = 0.04

NZ, NC, NY, NX = 8, 2, 4, 4
BLOCKS = 16
SAMP = 64
HALF = 128
QUARTER = 64
TOTAL = 1024
CHUNKS = 12
SLOTS = 8
LAGS = (1, 3, 5, 7)
MESH = pl.DeviceIdType.MESH
bf16, f32 = jnp.bfloat16, jnp.float32


PARTS = (("x", 1), ("x", -1), ("y", 1), ("y", -1))


def turned(value):
    return pltpu.roll(value.astype(f32), QUARTER, axis=value.ndim - 1)


def low_lanes(shape):
    return lax.broadcasted_iota(jnp.int32, shape, len(shape) - 1) < QUARTER


def kernel(x_ref, w_ref, pat_ref, count_ref, cand_ref, out_ref,
           xg, pga, pgb, pg1, own_p, wg, wt, at, hold, terms, fwd1, part, fwd2, m1, m23, n1, n23,
           x_rs, x_ss, xp_rs, xp_ss, w_rs, w_ss, p_rs, p_ss, pp_rs, pp_ss,
           m1_rs, m23_rs, n1_rs, n23_rs, t_ss, r_ss):
    v = lax.axis_index("var")
    l = lax.axis_index("layer")
    z, core = v // NC, v % NC
    y, x = l // NX, l % NX
    here = {"x": x, "y": y}

    def at_z(step):
        return {"var": ((z + step + NZ) % NZ) * NC + core, "layer": l}

    def at_xy(axis, step):
        if axis == "x":
            return {"var": v, "layer": y * NX + (x + step + NX) % NX}
        return {"var": v, "layer": ((y + step + NY) % NY) * NX + x}

    partner = {"var": z * NC + (1 - core), "layer": l}

    barrier = pltpu.get_barrier_semaphore()
    greeted = [at_z(1), at_z(-1), partner, at_xy("x", 1), at_xy("x", -1), at_xy("y", 1), at_xy("y", -1)]
    for device in greeted:
        pl.semaphore_signal(barrier, inc=1, device_id=device, device_id_type=MESH)

    for j in range(BLOCKS):
        for h in range(2):
            start = (j * 2 + h) * HALF
            xg[v * BLOCKS + j, h] = x_ref[:, start:start + HALF]
    pl.semaphore_wait(barrier, len(greeted))

    def push(src, dst, ss, rs, device):
        pltpu.make_async_remote_copy(src_ref=src, dst_ref=dst, send_sem=ss, recv_sem=rs,
                                     device_id=device, device_id_type=MESH).start()

    def arrived(ref, sem):
        pltpu.make_async_copy(ref, ref, sem).wait()

    def x_piece(vsrc, p):
        return xg.at[pl.ds(vsrc * BLOCKS + p * 4, 4)]

    def x_ring(vsrc, p, sign, hop):
        ref = x_piece(vsrc, p)
        push(ref, ref, x_ss, x_rs.at[0 if sign > 0 else 1, hop - 1, p], at_z(sign))

    def x_hop(h):
        for p in range(4):
            for sign in (1, -1):
                last = 4 if (p < 2) == (sign > 0) else 3
                if h > last:
                    continue
                vsrc = ((z - sign * h + NZ) % NZ) * NC + core
                ref = x_piece(vsrc, p)
                arrived(ref, x_rs.at[0 if sign > 0 else 1, h - 1, p])
                if h < last:
                    x_ring(vsrc, p, sign, h + 1)
                push(ref, ref, xp_ss, xp_rs, partner)

    for p in range(4):
        for sign in (1, -1):
            x_ring(v, p, sign, 1)

    def w_piece(lsrc, q):
        return wg.at[lsrc, q]

    def w_send(lsrc, q, axis, step):
        ref = w_piece(lsrc, q)
        push(ref, ref, w_ss, w_rs.at[q, lsrc], at_xy(axis, step))

    def w_wait(lsrc, q):
        arrived(w_piece(lsrc, q), w_rs.at[q, lsrc])

    def other(axis):
        return "y" if axis == "x" else "x"

    def l_at(first, a, second, b):
        pos = dict(here)
        pos[first] = (pos[first] + a + 4) % 4
        pos[second] = (pos[second] + b + 4) % 4
        return pos["y"] * NX + pos["x"]

    def each():
        for q, (d1, s) in enumerate(PARTS):
            yield q, d1, other(d1), s

    for q, d1, d2, s in each():
        def load(i4, carry, q=q):
            i = q * 4 + i4
            for k in range(4):
                rows = w_ref[:, i, k, :]
                wt[i, k] = rows
                wg[l, q, i4, k] = jnp.where(k < count_ref[i], rows, 0.0).astype(bf16)
            return carry

        lax.fori_loop(0, 4, load, 0)
        for step in (1, -1):
            w_send(l, q, d1, step)
    for q, d1, d2, s in each():
        for step in (1, -1):
            w_send(l, q, d2, step)
    push(xg.at[pl.ds(v * BLOCKS, BLOCKS)], xg.at[pl.ds(v * BLOCKS, BLOCKS)], xp_ss, xp_rs, partner)

    for q, d1, d2, s in each():
        for a in (-s, s):
            lsrc = l_at(d1, a, d2, 0)
            w_wait(lsrc, q)
            if a == -s:
                w_send(lsrc, q, d1, s)
            for step in (1, -1):
                w_send(lsrc, q, d2, step)
    x_hop(1)
    for q, d1, d2, s in each():
        for b in (-s, s):
            lsrc = l_at(d1, 0, d2, b)
            w_wait(lsrc, q)
            if b == -s:
                w_send(lsrc, q, d2, s)
    for q, d1, d2, s in each():
        lsrc = l_at(d1, 2, d2, 0)
        w_wait(lsrc, q)
        for step in (1, -1):
            w_send(lsrc, q, d2, step)
    x_hop(2)
    for a in (-1, 1, 2):
        for q, d1, d2, s in each():
            for b in (-s, s):
                lsrc = l_at(d1, a, d2, b)
                w_wait(lsrc, q)
                if b == -s:
                    w_send(lsrc, q, d2, s)
        if a == 1:
            x_hop(3)
    x_hop(4)
    arrived(xg.at[pl.ds(0, NZ * BLOCKS)], xp_rs)
    for a in (0, -1, 1, 2):
        for q, d1, d2, s in each():
            w_wait(l_at(d1, a, d2, 2), q)

    def product(i, carry):
        total = jnp.zeros((SAMP, 2 * HALF), f32)
        for k in range(4):
            j = pat_ref[k, i]
            cols = jnp.concatenate([xg[j, 0], xg[j, 1]], axis=1)
            rows = wg[:, i // 4, i % 4, k].reshape(2 * HALF, 2 * HALF)
            total += lax.dot_general(cols, rows, (((1,), (1,)), ((), ())), preferred_element_type=f32)
        result = total.astype(bf16)
        left = total[:, :HALF]
        other_half = turned(left)
        low = low_lanes((SAMP // 2, HALF))
        pga[v * BLOCKS + i] = jnp.where(low, left[:SAMP // 2], other_half[SAMP // 2:]).astype(bf16)
        pgb[v * BLOCKS + i] = jnp.where(low, other_half[:SAMP // 2], left[SAMP // 2:]).astype(bf16)
        own_p[i] = result[:, :HALF]
        pg1[v * BLOCKS + i] = result[:, HALF:]
        own = jnp.concatenate([xg[v * BLOCKS + i, 0], xg[v * BLOCKS + i, 1]], axis=1)
        both = jnp.concatenate([own.astype(f32), result.astype(f32)], axis=0)
        at[i] = both.T.astype(bf16)
        return carry

    lax.fori_loop(0, BLOCKS, product, 0)

    gathers = (pga, pgb, pg1)

    def p_piece(g, vsrc, p):
        return gathers[g].at[pl.ds(vsrc * BLOCKS + p * 8, 8)]

    def p_ring(g, vsrc, p, sign, hop):
        ref = p_piece(g, vsrc, p)
        push(ref, ref, p_ss.at[g], p_rs.at[g, 0 if sign > 0 else 1, hop - 1, p], at_z(sign))

    def p_start(g):
        for p in range(2):
            for sign in (1, -1):
                p_ring(g, v, p, sign, 1)
        ref = gathers[g].at[pl.ds(v * BLOCKS, BLOCKS)]
        push(ref, ref, pp_ss.at[g], pp_rs.at[g], partner)

    def p_hop(g, h):
        for p in range(2):
            for sign in (1, -1):
                last = 4 if (p == 0) == (sign > 0) else 3
                if h > last:
                    continue
                vsrc = ((z - sign * h + NZ) % NZ) * NC + core
                ref = p_piece(g, vsrc, p)
                arrived(ref, p_rs.at[g, 0 if sign > 0 else 1, h - 1, p])
                if h < last:
                    p_ring(g, vsrc, p, sign, h + 1)
                push(ref, ref, pp_ss.at[g], pp_rs.at[g], partner)
        if h == 4:
            arrived(gathers[g].at[pl.ds(0, NZ * BLOCKS)], pp_rs.at[g])

    def place(axis, step):
        return (here[axis] + step + 4) % 4

    def right_own(u, i):
        if u == 0:
            return jnp.concatenate([own_p[i], xg[v * BLOCKS + i, 0]], axis=0)
        return jnp.concatenate([pg1[v * BLOCKS + i], xg[v * BLOCKS + i, 1]], axis=0)

    def right_pair(u, i, second):
        base = 2 * u - (7 if second else 3)
        j, k = cand_ref[base, i], cand_ref[base + 1, i]
        pg = pgb if second else pga
        low = low_lanes((SAMP // 2, HALF))
        pj, pk, xj, xk = pg[j], pg[k], xg[j, 0], xg[k, 0]
        top = jnp.where(low, pj.astype(f32), turned(pk))
        bottom = jnp.where(low, turned(pj), pk.astype(f32))
        low = low_lanes((SAMP, HALF))
        if second:
            cols = jnp.where(low, turned(xj), xk.astype(f32))
        else:
            cols = jnp.where(low, xj.astype(f32), turned(xk))
        return jnp.concatenate([top, bottom, cols], axis=0).astype(bf16)

    def right_five(u, i):
        j = cand_ref[5, i]
        pa, pb = pga[j], pgb[j]
        low = low_lanes((SAMP // 2, HALF))
        top = jnp.where(low, pa.astype(f32), turned(pb))
        bottom = jnp.where(low, turned(pa), pb.astype(f32))
        return jnp.concatenate([top.astype(bf16), bottom.astype(bf16), xg[j, 0]], axis=0)

    def right_second(u, i):
        j = cand_ref[u - 6, i]
        return jnp.concatenate([pg1[j], xg[j, 1]], axis=0)

    def stage0(u, right):
        slot = u % SLOTS
        for q, d1, d2, s in each():
            for i4 in range(4):
                i = q * 4 + i4
                term = jnp.dot(at[i], right(u, i), preferred_element_type=f32).astype(bf16)
                for a in range(4):
                    for b in range(4):
                        row = 16 * ((b * NX + a) if d1 == "x" else (a * NX + b))
                        terms[slot, q, a, b, i4] = term[row:row + 16]
            push(terms.at[slot, q, place(d1, 2)], m1.at[u, q], t_ss.at[slot], m1_rs.at[u], at_xy(d1, s))
            push(terms.at[slot, q, place(d1, -s)], m23.at[u, q, 0], t_ss.at[slot], m23_rs.at[u], at_xy(d1, -s))

    def stage1(u):
        slot = u % SLOTS
        arrived(m1.at[u], m1_rs.at[u])
        for q, d1, d2, s in each():
            fwd1[slot, q] = (terms[slot, q, place(d1, s)].astype(f32) + m1[u, q].astype(f32)).astype(bf16)
            push(fwd1.at[slot, q], m23.at[u, q, 1], t_ss.at[slot], m23_rs.at[u], at_xy(d1, s))

    def stage2(u):
        slot = u % SLOTS
        arrived(m23.at[u], m23_rs.at[u])
        for q, d1, d2, s in each():
            part[slot, q] = (terms[slot, q, place(d1, 0)].astype(f32) + m23[u, q, 0].astype(f32)
                             + m23[u, q, 1].astype(f32)).astype(bf16)
            push(part.at[slot, q, place(d2, 2)], n1.at[u, q], r_ss.at[slot], n1_rs.at[u], at_xy(d2, s))
            push(part.at[slot, q, place(d2, -s)], n23.at[u, q, 0], r_ss.at[slot], n23_rs.at[u], at_xy(d2, -s))

    def stage3(u):
        slot = u % SLOTS
        arrived(n1.at[u], n1_rs.at[u])
        for q, d1, d2, s in each():
            fwd2[slot, q] = (part[slot, q, place(d2, s)].astype(f32) + n1[u, q].astype(f32)).astype(bf16)
            push(fwd2.at[slot, q], n23.at[u, q, 1], r_ss.at[slot], n23_rs.at[u], at_xy(d2, s))

    def finish(i, c, qh, total):
        columns = pl.ds(qh * HALF, HALF)
        j = cand_ref[c, i]
        live = count_ref[i]
        slot, found = 0, 0
        for k in range(4):
            match = jnp.where((pat_ref[k, i] == j) & (k < live), 1, 0)
            slot, found = slot + k * match, found + match
        previous = jnp.where(found > 0, wt[i, slot, :, columns], 0.0)
        stepped = previous - step_size * (total * (1.0 / (2.0 * TOTAL)))
        size = jnp.maximum(jnp.abs(stepped) - step_size * penalty, 0.0)
        result = jnp.where(stepped < 0, -size, size)
        if isinstance(c, int) and c == 0:
            rows = l * 16 + lax.broadcasted_iota(jnp.int32, (16, HALF), 0)
            cols = qh * HALF + lax.broadcasted_iota(jnp.int32, (16, HALF), 1)
            on = rows == cols
            diagonal = jnp.where(on, wt[i, 0, :, columns], 1.0)
            result = jnp.where(on, stepped + step_size * (1.0 / diagonal), result)
        out_ref[:, c, i, columns] = result

    def stage4(u, kind):
        slot = u % SLOTS
        arrived(n23.at[u], n23_rs.at[u])
        low = low_lanes((16, HALF))
        for q, d1, d2, s in each():
            for i4 in range(4):
                i = q * 4 + i4
                total = (part[slot, q, place(d2, 0), i4].astype(f32) + n23[u, q, 0, i4].astype(f32)
                         + n23[u, q, 1, i4].astype(f32))
                if kind == "own":
                    finish(i, 0, u, total)
                elif kind == "first":
                    hold[u - 2, i] = total
                elif kind == "pair":
                    before = hold[u - 4, i]
                    finish(i, 2 * u - 7, 0, jnp.where(low, before, turned(total)))
                    finish(i, 2 * u - 6, 0, jnp.where(low, turned(before), total))
                elif kind == "five":
                    finish(i, 5, 0, total)
                else:
                    finish(i, u - 6, 1, total)
        arrived(terms.at[slot, pl.ds(0, 3)], t_ss.at[slot])
        arrived(part.at[slot, pl.ds(0, 3)], r_ss.at[slot])

    p_start(0)
    stage0(0, right_own)
    stage0(1, right_own)
    p_hop(0, 1)
    stage1(0)
    p_hop(0, 2)
    stage1(1)
    p_hop(0, 3)
    p_start(1)
    stage2(0)
    p_hop(0, 4)
    stage2(1)

    def turn(u, carry):
        def when(low, high, what):
            pl.when((u >= low) & (u < high))(what)

        def hops(*steps):
            def run():
                for g, h in steps:
                    p_hop(g, h)
                    if (g, h) == (1, 3):
                        p_start(2)
            return run

        when(4, 5, hops((1, 4)))
        when(7, 8, hops((2, 4)))
        when(2, 4, lambda: stage0(u, lambda u, i: right_pair(u, i, False)))
        when(4, 6, lambda: stage0(u, lambda u, i: right_pair(u, i, True)))
        when(6, 7, lambda: stage0(u, right_five))
        when(7, 12, lambda: stage0(u, right_second))
        a, b, c, d = LAGS
        when(2 + a, 12 + a, lambda: stage1(u - a))
        when(2 + b, 12 + b, lambda: stage2(u - b))
        when(c, 12 + c, lambda: stage3(u - c))
        when(d, d + 1, lambda: stage4(0, "own"))
        when(d + 1, d + 2, lambda: stage4(1, "own"))
        when(d + 2, d + 4, lambda: stage4(u - d, "first"))
        when(d + 4, d + 6, lambda: stage4(u - d, "pair"))
        when(d + 6, d + 7, lambda: stage4(u - d, "five"))
        when(d + 7, d + 12, lambda: stage4(u - d, "second"))
        when(2, 3, hops((1, 1), (1, 2)))
        when(3, 4, hops((1, 3)))
        when(4, 5, hops((2, 1)))
        when(5, 6, hops((2, 2)))
        when(6, 7, hops((2, 3)))
        return carry

    lax.fori_loop(2, CHUNKS + LAGS[3], turn, 0)

    arrived(xg.at[pl.ds(0, 7 * BLOCKS)], x_ss)
    arrived(xg.at[pl.ds(0, 8 * BLOCKS)], xp_ss)
    arrived(wg.at[pl.ds(0, 15)], w_ss)
    for g in range(3):
        arrived(gathers[g].at[pl.ds(0, 7 * BLOCKS)], p_ss.at[g])
        arrived(gathers[g].at[pl.ds(0, 8 * BLOCKS)], pp_ss.at[g])


def body(sample_matrix, precision_blocks, block_pattern, block_counts, candidate_cols):
    vmem = pl.BlockSpec(memory_space=pltpu.VMEM)
    smem = pl.BlockSpec(memory_space=pltpu.SMEM)
    dma = pltpu.SemaphoreType.DMA
    scratch = [
        pltpu.VMEM((256, 2, SAMP, HALF), bf16),
        pltpu.VMEM((256, SAMP // 2, HALF), bf16),
        pltpu.VMEM((256, SAMP // 2, HALF), bf16),
        pltpu.VMEM((256, SAMP, HALF), bf16),
        pltpu.VMEM((BLOCKS, SAMP, HALF), bf16),
        pltpu.VMEM((16, 4, 4, 4, 16, 256), bf16),
        pltpu.VMEM((BLOCKS, 4, 16, 256), f32),
        pltpu.VMEM((BLOCKS, 256, 128), bf16),
        pltpu.VMEM((2, BLOCKS, 16, HALF), f32),
        pltpu.VMEM((SLOTS, 4, 4, 4, 4, 16, HALF), bf16),
        pltpu.VMEM((SLOTS, 4, 4, 4, 16, HALF), bf16),
        pltpu.VMEM((SLOTS, 4, 4, 4, 16, HALF), bf16),
        pltpu.VMEM((SLOTS, 4, 4, 16, HALF), bf16),
        pltpu.VMEM((CHUNKS, 4, 4, 4, 16, HALF), bf16),
        pltpu.VMEM((CHUNKS, 4, 2, 4, 4, 16, HALF), bf16),
        pltpu.VMEM((CHUNKS, 4, 4, 16, HALF), bf16),
        pltpu.VMEM((CHUNKS, 4, 2, 4, 16, HALF), bf16),
        dma((2, 4, 4)), dma(()), dma(()), dma(()),
        dma((4, 16)), dma(()),
        dma((3, 2, 4, 2)), dma((3,)), dma((3,)), dma((3,)),
        dma((CHUNKS,)), dma((CHUNKS,)), dma((CHUNKS,)), dma((CHUNKS,)), dma((SLOTS,)), dma((SLOTS,)),
    ]
    updated = pl.pallas_call(
        kernel,
        out_shape=jax.ShapeDtypeStruct((16, 6, BLOCKS, 2 * HALF), f32),
        in_specs=[vmem, vmem, smem, smem, smem],
        out_specs=vmem,
        scratch_shapes=scratch,
        compiler_params=pltpu.CompilerParams(
            collective_id=0, has_side_effects=True, vmem_limit_bytes=60 * 2 ** 20),
    )(sample_matrix, precision_blocks, block_pattern.T, block_counts, candidate_cols.T)
    return jnp.transpose(updated, (0, 2, 1, 3))


def solution(mesh):
    placed = (
        P("layer", "var"),
        P("layer", "var", None, None),
        P("var", None),
        P("var"),
        P("var", None),
    )
    return jax.shard_map(
        body, mesh=mesh, in_specs=placed, out_specs=P("layer", "var", None, None), check_vma=False
    )
```

```python
import jax
import jax.numpy as jnp
from jax import lax
from jax.experimental import pallas as pl
from jax.experimental.pallas import tpu as pltpu
from jax.sharding import PartitionSpec as P

step_size = 0.5
penalty = 0.04

NZ, NC, NY, NX = 8, 2, 4, 4
BLOCKS = 16
SAMP = 64
HALF = 128
QUARTER = 64
TOTAL = 1024
CHUNKS = 12
PIECES = 4
SLOTS = 8
LAGS = (1, 3, 5, 7)
MESH = pl.DeviceIdType.MESH
bf16, f32 = jnp.bfloat16, jnp.float32


PARTS = (("x", 1), ("x", -1), ("y", 1), ("y", -1))


def turned(value):
    return pltpu.roll(value.astype(f32), QUARTER, axis=value.ndim - 1)


def low_lanes(shape):
    return lax.broadcasted_iota(jnp.int32, shape, len(shape) - 1) < QUARTER


def kernel(x_ref, w_ref, pat_ref, count_ref, cand_ref, out_ref,
           xg, pga, pgb, pg1, own_p, wg, wt, at, hold, terms, fwd1, part, fwd2, m1, m23, n1, n23,
           x_rs, x_ss, xp_rs, xp_ss, w_rs, w_ss, p_rs, p_ss, pp_rs, pp_ss,
           m1_rs, m23_rs, n1_rs, n23_rs, t_ss, r_ss):
    v = lax.axis_index("var")
    l = lax.axis_index("layer")
    z, core = v // NC, v % NC
    y, x = l // NX, l % NX
    here = {"x": x, "y": y}

    def at_z(step):
        return {"var": ((z + step + NZ) % NZ) * NC + core, "layer": l}

    def at_xy(axis, step):
        if axis == "x":
            return {"var": v, "layer": y * NX + (x + step + NX) % NX}
        return {"var": v, "layer": ((y + step + NY) % NY) * NX + x}

    partner = {"var": z * NC + (1 - core), "layer": l}

    barrier = pltpu.get_barrier_semaphore()
    greeted = [at_z(1), at_z(-1), partner, at_xy("x", 1), at_xy("x", -1), at_xy("y", 1), at_xy("y", -1)]
    for device in greeted:
        pl.semaphore_signal(barrier, inc=1, device_id=device, device_id_type=MESH)

    for j in range(BLOCKS):
        for h in range(2):
            start = (j * 2 + h) * HALF
            xg[v * BLOCKS + j, h] = x_ref[:, start:start + HALF]
    pl.semaphore_wait(barrier, len(greeted))

    def push(src, dst, ss, rs, device):
        pltpu.make_async_remote_copy(src_ref=src, dst_ref=dst, send_sem=ss, recv_sem=rs,
                                     device_id=device, device_id_type=MESH).start()

    def arrived(ref, sem):
        pltpu.make_async_copy(ref, ref, sem).wait()

    def x_piece(vsrc, p):
        return xg.at[pl.ds(vsrc * BLOCKS + p * 4, 4)]

    def x_ring(vsrc, p, sign, hop):
        ref = x_piece(vsrc, p)
        push(ref, ref, x_ss, x_rs.at[0 if sign > 0 else 1, hop - 1, p], at_z(sign))

    def x_hop(h, pieces=range(4)):
        for p in pieces:
            for sign in (1, -1):
                last = 4 if (p < 2) == (sign > 0) else 3
                if h > last:
                    continue
                vsrc = ((z - sign * h + NZ) % NZ) * NC + core
                ref = x_piece(vsrc, p)
                arrived(ref, x_rs.at[0 if sign > 0 else 1, h - 1, p])
                if h < last:
                    x_ring(vsrc, p, sign, h + 1)
                push(ref, ref, xp_ss, xp_rs, partner)

    for p in range(4):
        for sign in (1, -1):
            x_ring(v, p, sign, 1)

    def w_piece(lsrc, q):
        return wg.at[lsrc, q]

    def w_send(lsrc, q, axis, step):
        ref = w_piece(lsrc, q)
        push(ref, ref, w_ss, w_rs.at[q, lsrc], at_xy(axis, step))

    def w_wait(lsrc, q):
        arrived(w_piece(lsrc, q), w_rs.at[q, lsrc])

    def other(axis):
        return "y" if axis == "x" else "x"

    def l_at(first, a, second, b):
        pos = dict(here)
        pos[first] = (pos[first] + a + 4) % 4
        pos[second] = (pos[second] + b + 4) % 4
        return pos["y"] * NX + pos["x"]

    def each():
        for q, (d1, s) in enumerate(PARTS):
            yield q, d1, other(d1), s

    for q, d1, d2, s in each():
        def load(i4, carry, q=q):
            i = q * 4 + i4
            for k in range(4):
                rows = w_ref[:, i, k, :]
                wt[i, k] = rows
                wg[l, q, i4, k] = jnp.where(k < count_ref[i], rows, 0.0).astype(bf16)
            return carry

        lax.fori_loop(0, 4, load, 0)
        for step in (1, -1):
            w_send(l, q, d1, step)
    for q, d1, d2, s in each():
        for step in (1, -1):
            w_send(l, q, d2, step)
    push(xg.at[pl.ds(v * BLOCKS, BLOCKS)], xg.at[pl.ds(v * BLOCKS, BLOCKS)], xp_ss, xp_rs, partner)

    def w_first(parts=PARTS):
        for q, d1, d2, s in each():
            if PARTS[q] not in parts:
                continue
            for a in (-s, s):
                lsrc = l_at(d1, a, d2, 0)
                w_wait(lsrc, q)
                if a == -s:
                    w_send(lsrc, q, d1, s)
                for step in (1, -1):
                    w_send(lsrc, q, d2, step)

    def w_long():
        for q, d1, d2, s in each():
            lsrc = l_at(d1, 2, d2, 0)
            w_wait(lsrc, q)
            for step in (1, -1):
                w_send(lsrc, q, d2, step)

    def w_second(a):
        for q, d1, d2, s in each():
            for b in (-s, s):
                lsrc = l_at(d1, a, d2, b)
                w_wait(lsrc, q)
                if b == -s:
                    w_send(lsrc, q, d2, s)

    x_hop(1, (0, 2))
    w_first()
    x_hop(1, (1, 3))
    w_second(0)
    x_hop(2, (0, 2))
    w_long()
    x_hop(2, (1, 3))
    w_second(-1)
    x_hop(3, (0, 2))
    w_second(1)
    x_hop(3, (1, 3))
    w_second(2)
    x_hop(4)
    arrived(xg.at[pl.ds(0, NZ * BLOCKS)], xp_rs)
    for a in (0, -1, 1, 2):
        for q, d1, d2, s in each():
            w_wait(l_at(d1, a, d2, 2), q)

    def product(i, carry):
        total = jnp.zeros((SAMP, 2 * HALF), f32)
        for k in range(4):
            j = pat_ref[k, i]
            cols = jnp.concatenate([xg[j, 0], xg[j, 1]], axis=1)
            rows = wg[:, i // 4, i % 4, k].reshape(2 * HALF, 2 * HALF)
            total += lax.dot_general(cols, rows, (((1,), (1,)), ((), ())), preferred_element_type=f32)
        result = total.astype(bf16)
        left = total[:, :HALF]
        other_half = turned(left)
        low = low_lanes((SAMP // 2, HALF))
        pga[v * BLOCKS + i] = jnp.where(low, left[:SAMP // 2], other_half[SAMP // 2:]).astype(bf16)
        pgb[v * BLOCKS + i] = jnp.where(low, other_half[:SAMP // 2], left[SAMP // 2:]).astype(bf16)
        own_p[i] = result[:, :HALF]
        pg1[v * BLOCKS + i] = result[:, HALF:]
        own = jnp.concatenate([xg[v * BLOCKS + i, 0], xg[v * BLOCKS + i, 1]], axis=1)
        both = jnp.concatenate([own.astype(f32), result.astype(f32)], axis=0)
        at[i] = both.T.astype(bf16)
        return carry


    gathers = (pga, pgb, pg1)

    def p_piece(g, vsrc, p):
        rows = BLOCKS // PIECES
        return gathers[g].at[pl.ds(vsrc * BLOCKS + p * rows, rows)]

    def p_ring(g, vsrc, p, sign, hop):
        ref = p_piece(g, vsrc, p)
        push(ref, ref, p_ss.at[g], p_rs.at[g, 0 if sign > 0 else 1, hop - 1, p], at_z(sign))

    def p_first(g, p):
        for sign in (1, -1):
            p_ring(g, v, p, sign, 1)
        ref = p_piece(g, v, p)
        push(ref, ref, pp_ss.at[g], pp_rs.at[g], partner)

    def p_start(g):
        for p in range(PIECES):
            p_first(g, p)

    def p_hop(g, h):
        for p in range(PIECES):
            for sign in (1, -1):
                last = 4 if (p % 2 == 0) == (sign > 0) else 3
                if h > last:
                    continue
                vsrc = ((z - sign * h + NZ) % NZ) * NC + core
                ref = p_piece(g, vsrc, p)
                arrived(ref, p_rs.at[g, 0 if sign > 0 else 1, h - 1, p])
                if h < last:
                    p_ring(g, vsrc, p, sign, h + 1)
                push(ref, ref, pp_ss.at[g], pp_rs.at[g], partner)
        if h == 4:
            arrived(gathers[g].at[pl.ds(0, NZ * BLOCKS)], pp_rs.at[g])

    def place(axis, step):
        return (here[axis] + step + 4) % 4

    def right_own(u, i):
        if u == 0:
            return jnp.concatenate([own_p[i], xg[v * BLOCKS + i, 0]], axis=0)
        return jnp.concatenate([pg1[v * BLOCKS + i], xg[v * BLOCKS + i, 1]], axis=0)

    def right_pair(u, i, second):
        base = 2 * u - (7 if second else 3)
        j, k = cand_ref[base, i], cand_ref[base + 1, i]
        pg = pgb if second else pga
        low = low_lanes((SAMP // 2, HALF))
        pj, pk, xj, xk = pg[j], pg[k], xg[j, 0], xg[k, 0]
        top = jnp.where(low, pj.astype(f32), turned(pk))
        bottom = jnp.where(low, turned(pj), pk.astype(f32))
        low = low_lanes((SAMP, HALF))
        if second:
            cols = jnp.where(low, turned(xj), xk.astype(f32))
        else:
            cols = jnp.where(low, xj.astype(f32), turned(xk))
        return jnp.concatenate([top, bottom, cols], axis=0).astype(bf16)

    def right_five(u, i):
        j = cand_ref[5, i]
        pa, pb = pga[j], pgb[j]
        low = low_lanes((SAMP // 2, HALF))
        top = jnp.where(low, pa.astype(f32), turned(pb))
        bottom = jnp.where(low, turned(pa), pb.astype(f32))
        return jnp.concatenate([top.astype(bf16), bottom.astype(bf16), xg[j, 0]], axis=0)

    def right_second(u, i):
        j = cand_ref[u - 6, i]
        return jnp.concatenate([pg1[j], xg[j, 1]], axis=0)

    def stage0(u, right, parts=range(4)):
        slot = u % SLOTS
        for q, d1, d2, s in each():
            if q not in parts:
                continue
            for i4 in range(4):
                i = q * 4 + i4
                term = jnp.dot(at[i], right(u, i), preferred_element_type=f32).astype(bf16)
                for a in range(4):
                    for b in range(4):
                        row = 16 * ((b * NX + a) if d1 == "x" else (a * NX + b))
                        terms[slot, q, a, b, i4] = term[row:row + 16]
            push(terms.at[slot, q, place(d1, 2)], m1.at[u, q], t_ss.at[slot], m1_rs.at[u], at_xy(d1, s))
            push(terms.at[slot, q, place(d1, -s)], m23.at[u, q, 0], t_ss.at[slot], m23_rs.at[u], at_xy(d1, -s))

    def stage1(u):
        slot = u % SLOTS
        arrived(m1.at[u], m1_rs.at[u])
        for q, d1, d2, s in each():
            fwd1[slot, q] = (terms[slot, q, place(d1, s)].astype(f32) + m1[u, q].astype(f32)).astype(bf16)
            push(fwd1.at[slot, q], m23.at[u, q, 1], t_ss.at[slot], m23_rs.at[u], at_xy(d1, s))

    def stage2(u):
        slot = u % SLOTS
        arrived(m23.at[u], m23_rs.at[u])
        for q, d1, d2, s in each():
            part[slot, q] = (terms[slot, q, place(d1, 0)].astype(f32) + m23[u, q, 0].astype(f32)
                             + m23[u, q, 1].astype(f32)).astype(bf16)
            push(part.at[slot, q, place(d2, 2)], n1.at[u, q], r_ss.at[slot], n1_rs.at[u], at_xy(d2, s))
            push(part.at[slot, q, place(d2, -s)], n23.at[u, q, 0], r_ss.at[slot], n23_rs.at[u], at_xy(d2, -s))

    def stage3(u):
        slot = u % SLOTS
        arrived(n1.at[u], n1_rs.at[u])
        for q, d1, d2, s in each():
            fwd2[slot, q] = (part[slot, q, place(d2, s)].astype(f32) + n1[u, q].astype(f32)).astype(bf16)
            push(fwd2.at[slot, q], n23.at[u, q, 1], r_ss.at[slot], n23_rs.at[u], at_xy(d2, s))

    def finish(i, c, qh, total):
        columns = pl.ds(qh * HALF, HALF)
        j = cand_ref[c, i]
        live = count_ref[i]
        slot, found = 0, 0
        for k in range(4):
            match = jnp.where((pat_ref[k, i] == j) & (k < live), 1, 0)
            slot, found = slot + k * match, found + match
        previous = jnp.where(found > 0, wt[i, slot, :, columns], 0.0)
        stepped = previous - step_size * (total * (1.0 / (2.0 * TOTAL)))
        size = jnp.maximum(jnp.abs(stepped) - step_size * penalty, 0.0)
        result = jnp.where(stepped < 0, -size, size)
        if isinstance(c, int) and c == 0:
            rows = l * 16 + lax.broadcasted_iota(jnp.int32, (16, HALF), 0)
            cols = qh * HALF + lax.broadcasted_iota(jnp.int32, (16, HALF), 1)
            on = rows == cols
            diagonal = jnp.where(on, wt[i, 0, :, columns], 1.0)
            result = jnp.where(on, stepped + step_size * (1.0 / diagonal), result)
        out_ref[:, c, i, columns] = result

    def stage4(u, kind):
        slot = u % SLOTS
        arrived(n23.at[u], n23_rs.at[u])
        low = low_lanes((16, HALF))
        for q, d1, d2, s in each():
            for i4 in range(4):
                i = q * 4 + i4
                total = (part[slot, q, place(d2, 0), i4].astype(f32) + n23[u, q, 0, i4].astype(f32)
                         + n23[u, q, 1, i4].astype(f32))
                if kind == "own":
                    finish(i, 0, u, total)
                elif kind == "first":
                    hold[u - 2, i] = total
                elif kind == "pair":
                    before = hold[u - 4, i]
                    finish(i, 2 * u - 7, 0, jnp.where(low, before, turned(total)))
                    finish(i, 2 * u - 6, 0, jnp.where(low, turned(before), total))
                elif kind == "five":
                    finish(i, 5, 0, total)
                else:
                    finish(i, u - 6, 1, total)
        arrived(terms.at[slot, pl.ds(0, 3)], t_ss.at[slot])
        arrived(part.at[slot, pl.ds(0, 3)], r_ss.at[slot])

    for q in range(4):
        lax.fori_loop(q * 4, q * 4 + 4, product, 0, unroll=4)
        p_first(0, q)
        stage0(0, right_own, (q,))
        stage0(1, right_own, (q,))
    p_hop(0, 1)
    stage1(0)
    p_start(1)
    p_hop(0, 2)
    stage1(1)
    p_hop(1, 1)
    p_hop(0, 3)
    stage2(0)
    p_hop(1, 2)
    p_hop(0, 4)
    p_start(2)
    stage2(1)
    p_hop(1, 3)

    def turn(u, carry):
        def when(low, high, what):
            pl.when((u >= low) & (u < high))(what)

        def hops(at, *steps):
            @pl.when(u == at)
            def _():
                for g, h in steps:
                    p_hop(g, h)
                    if (g, h) == (1, 3):
                        p_start(2)

        hops(4, (1, 4))
        hops(7, (2, 4))
        when(2, 4, lambda: stage0(u, lambda u, i: right_pair(u, i, False)))
        when(4, 6, lambda: stage0(u, lambda u, i: right_pair(u, i, True)))
        when(6, 7, lambda: stage0(u, right_five))
        when(7, 12, lambda: stage0(u, right_second))
        a, b, c, d = LAGS
        when(2 + a, 12 + a, lambda: stage1(u - a))
        when(2 + b, 12 + b, lambda: stage2(u - b))
        when(c, 12 + c, lambda: stage3(u - c))
        when(d, d + 1, lambda: stage4(0, "own"))
        when(d + 1, d + 2, lambda: stage4(1, "own"))
        when(d + 2, d + 4, lambda: stage4(u - d, "first"))
        when(d + 4, d + 6, lambda: stage4(u - d, "pair"))
        when(d + 6, d + 7, lambda: stage4(u - d, "five"))
        when(d + 7, d + 12, lambda: stage4(u - d, "second"))
        hops(3, (2, 1))
        hops(4, (2, 2))
        hops(5, (2, 3))
        return carry

    lax.fori_loop(2, CHUNKS + LAGS[3], turn, 0)

    arrived(xg.at[pl.ds(0, 7 * BLOCKS)], x_ss)
    arrived(xg.at[pl.ds(0, 8 * BLOCKS)], xp_ss)
    arrived(wg.at[pl.ds(0, 15)], w_ss)
    for g in range(3):
        arrived(gathers[g].at[pl.ds(0, 7 * BLOCKS)], p_ss.at[g])
        arrived(gathers[g].at[pl.ds(0, 8 * BLOCKS)], pp_ss.at[g])


def body(sample_matrix, precision_blocks, block_pattern, block_counts, candidate_cols):
    vmem = pl.BlockSpec(memory_space=pltpu.VMEM)
    smem = pl.BlockSpec(memory_space=pltpu.SMEM)
    dma = pltpu.SemaphoreType.DMA
    scratch = [
        pltpu.VMEM((256, 2, SAMP, HALF), bf16),
        pltpu.VMEM((256, SAMP // 2, HALF), bf16),
        pltpu.VMEM((256, SAMP // 2, HALF), bf16),
        pltpu.VMEM((256, SAMP, HALF), bf16),
        pltpu.VMEM((BLOCKS, SAMP, HALF), bf16),
        pltpu.VMEM((16, 4, 4, 4, 16, 256), bf16),
        pltpu.VMEM((BLOCKS, 4, 16, 256), f32),
        pltpu.VMEM((BLOCKS, 256, 128), bf16),
        pltpu.VMEM((2, BLOCKS, 16, HALF), f32),
        pltpu.VMEM((SLOTS, 4, 4, 4, 4, 16, HALF), bf16),
        pltpu.VMEM((SLOTS, 4, 4, 4, 16, HALF), bf16),
        pltpu.VMEM((SLOTS, 4, 4, 4, 16, HALF), bf16),
        pltpu.VMEM((SLOTS, 4, 4, 16, HALF), bf16),
        pltpu.VMEM((CHUNKS, 4, 4, 4, 16, HALF), bf16),
        pltpu.VMEM((CHUNKS, 4, 2, 4, 4, 16, HALF), bf16),
        pltpu.VMEM((CHUNKS, 4, 4, 16, HALF), bf16),
        pltpu.VMEM((CHUNKS, 4, 2, 4, 16, HALF), bf16),
        dma((2, 4, 4)), dma(()), dma(()), dma(()),
        dma((4, 16)), dma(()),
        dma((3, 2, 4, PIECES)), dma((3,)), dma((3,)), dma((3,)),
        dma((CHUNKS,)), dma((CHUNKS,)), dma((CHUNKS,)), dma((CHUNKS,)), dma((SLOTS,)), dma((SLOTS,)),
    ]
    updated = pl.pallas_call(
        kernel,
        out_shape=jax.ShapeDtypeStruct((16, 6, BLOCKS, 2 * HALF), f32),
        in_specs=[vmem, vmem, smem, smem, smem],
        out_specs=vmem,
        scratch_shapes=scratch,
        compiler_params=pltpu.CompilerParams(
            collective_id=0, has_side_effects=True, vmem_limit_bytes=60 * 2 ** 20),
    )(sample_matrix, precision_blocks, block_pattern.T, block_counts, candidate_cols.T)
    return jnp.transpose(updated, (0, 2, 1, 3))


def solution(mesh):
    placed = (
        P("layer", "var"),
        P("layer", "var", None, None),
        P("var", None),
        P("var"),
        P("var", None),
    )
    return jax.shard_map(
        body, mesh=mesh, in_specs=placed, out_specs=P("layer", "var", None, None), check_vma=False
    )
```

```python
import jax
import jax.numpy as jnp
from jax import lax
from jax.experimental import pallas as pl
from jax.experimental.pallas import tpu as pltpu
from jax.sharding import PartitionSpec as P

step_size = 0.5
penalty = 0.04

NZ, NC, NY, NX = 8, 2, 4, 4
BLOCKS = 16
SAMP = 64
HALF = 128
QUARTER = 64
TOTAL = 1024
CHUNKS = 12
PIECES = 4
SLOTS = 8
LAGS = (1, 3, 5, 7)
MESH = pl.DeviceIdType.MESH
bf16, f32 = jnp.bfloat16, jnp.float32


PARTS = (("x", 1), ("x", -1), ("y", 1), ("y", -1))


def turned(value):
    return pltpu.roll(value.astype(f32), QUARTER, axis=value.ndim - 1)


def low_lanes(shape):
    return lax.broadcasted_iota(jnp.int32, shape, len(shape) - 1) < QUARTER


def kernel(x_in, w_in, pat_ref, count_ref, cand_ref, out_ref,
           x_ref, w_ref, in_sem,
           xg, pga, pgb, pg1, own_p, wg, wt, at, hold, terms, fwd1, part, fwd2, m1, m23, n1, n23,
           x_rs, x_ss, xp_rs, xp_ss, w_rs, w_ss, p_rs, p_ss, pp_rs, pp_ss,
           m1_rs, m23_rs, n1_rs, n23_rs, t_ss, r_ss):
    v = lax.axis_index("var")
    l = lax.axis_index("layer")
    z, core = v // NC, v % NC
    y, x = l // NX, l % NX
    here = {"x": x, "y": y}

    def at_z(step):
        return {"var": ((z + step + NZ) % NZ) * NC + core, "layer": l}

    def at_xy(axis, step):
        if axis == "x":
            return {"var": v, "layer": y * NX + (x + step + NX) % NX}
        return {"var": v, "layer": ((y + step + NY) % NY) * NX + x}

    partner = {"var": z * NC + (1 - core), "layer": l}

    barrier = pltpu.get_barrier_semaphore()
    greeted = [at_z(1), at_z(-1), partner, at_xy("x", 1), at_xy("x", -1), at_xy("y", 1), at_xy("y", -1)]
    for device in greeted:
        pl.semaphore_signal(barrier, inc=1, device_id=device, device_id_type=MESH)

    x_copy = pltpu.make_async_copy(x_in, x_ref, in_sem.at[0])
    w_copy = pltpu.make_async_copy(w_in, w_ref, in_sem.at[1])
    x_copy.start()
    w_copy.start()

    x_copy.wait()
    for j in range(BLOCKS):
        for h in range(2):
            start = (j * 2 + h) * HALF
            xg[v * BLOCKS + j, h] = x_ref[:, start:start + HALF]
    pl.semaphore_wait(barrier, len(greeted))

    def push(src, dst, ss, rs, device):
        pltpu.make_async_remote_copy(src_ref=src, dst_ref=dst, send_sem=ss, recv_sem=rs,
                                     device_id=device, device_id_type=MESH).start()

    def arrived(ref, sem):
        pltpu.make_async_copy(ref, ref, sem).wait()

    def x_piece(vsrc, p):
        return xg.at[pl.ds(vsrc * BLOCKS + p * 4, 4)]

    def x_ring(vsrc, p, sign, hop):
        ref = x_piece(vsrc, p)
        push(ref, ref, x_ss, x_rs.at[0 if sign > 0 else 1, hop - 1, p], at_z(sign))

    def x_hop(h, pieces=range(4)):
        for p in pieces:
            for sign in (1, -1):
                last = 4 if (p < 2) == (sign > 0) else 3
                if h > last:
                    continue
                vsrc = ((z - sign * h + NZ) % NZ) * NC + core
                ref = x_piece(vsrc, p)
                arrived(ref, x_rs.at[0 if sign > 0 else 1, h - 1, p])
                if h < last:
                    x_ring(vsrc, p, sign, h + 1)
                push(ref, ref, xp_ss, xp_rs, partner)

    for p in range(4):
        for sign in (1, -1):
            x_ring(v, p, sign, 1)

    def w_piece(lsrc, q):
        return wg.at[lsrc, q]

    def w_send(lsrc, q, axis, step):
        ref = w_piece(lsrc, q)
        push(ref, ref, w_ss, w_rs.at[q, lsrc], at_xy(axis, step))

    def w_wait(lsrc, q):
        arrived(w_piece(lsrc, q), w_rs.at[q, lsrc])

    def other(axis):
        return "y" if axis == "x" else "x"

    def l_at(first, a, second, b):
        pos = dict(here)
        pos[first] = (pos[first] + a + 4) % 4
        pos[second] = (pos[second] + b + 4) % 4
        return pos["y"] * NX + pos["x"]

    def each():
        for q, (d1, s) in enumerate(PARTS):
            yield q, d1, other(d1), s

    w_copy.wait()
    for q, d1, d2, s in each():
        def load(i4, carry, q=q):
            i = q * 4 + i4
            for k in range(4):
                rows = w_ref[:, i, k, :]
                wt[i, k] = rows
                wg[l, q, i4, k] = jnp.where(k < count_ref[i], rows, 0.0).astype(bf16)
            return carry

        lax.fori_loop(0, 4, load, 0)
        for step in (1, -1):
            w_send(l, q, d1, step)
    for q, d1, d2, s in each():
        for step in (1, -1):
            w_send(l, q, d2, step)
    push(xg.at[pl.ds(v * BLOCKS, BLOCKS)], xg.at[pl.ds(v * BLOCKS, BLOCKS)], xp_ss, xp_rs, partner)

    def w_first(parts=PARTS):
        for q, d1, d2, s in each():
            if PARTS[q] not in parts:
                continue
            for a in (-s, s):
                lsrc = l_at(d1, a, d2, 0)
                w_wait(lsrc, q)
                if a == -s:
                    w_send(lsrc, q, d1, s)
                for step in (1, -1):
                    w_send(lsrc, q, d2, step)

    def w_long():
        for q, d1, d2, s in each():
            lsrc = l_at(d1, 2, d2, 0)
            w_wait(lsrc, q)
            for step in (1, -1):
                w_send(lsrc, q, d2, step)

    def w_second(a):
        for q, d1, d2, s in each():
            for b in (-s, s):
                lsrc = l_at(d1, a, d2, b)
                w_wait(lsrc, q)
                if b == -s:
                    w_send(lsrc, q, d2, s)

    x_hop(1, (0, 2))
    w_first()
    x_hop(1, (1, 3))
    w_second(0)
    x_hop(2, (0, 2))
    w_long()
    x_hop(2, (1, 3))
    w_second(-1)
    x_hop(3, (0, 2))
    w_second(1)
    x_hop(3, (1, 3))
    w_second(2)
    x_hop(4)
    arrived(xg.at[pl.ds(0, NZ * BLOCKS)], xp_rs)
    for a in (0, -1, 1, 2):
        for q, d1, d2, s in each():
            w_wait(l_at(d1, a, d2, 2), q)

    def product(i, half):
        total = jnp.zeros((SAMP, HALF), f32)
        for k in range(4):
            j = pat_ref[k, i]
            cols = jnp.concatenate([xg[j, 0], xg[j, 1]], axis=1)
            rows = wg[half * 8:half * 8 + 8, i // 4, i % 4, k].reshape(HALF, 2 * HALF)
            total += lax.dot_general(cols, rows, (((1,), (1,)), ((), ())), preferred_element_type=f32)
        return total

    def product_first(i, carry):
        left = product(i, 0)
        swapped = turned(left)
        low = low_lanes((SAMP // 2, HALF))
        pga[v * BLOCKS + i] = jnp.where(low, left[:SAMP // 2], swapped[SAMP // 2:]).astype(bf16)
        pgb[v * BLOCKS + i] = jnp.where(low, swapped[:SAMP // 2], left[SAMP // 2:]).astype(bf16)
        own_p[i] = left.astype(bf16)
        return carry

    def product_second(i, carry):
        result = product(i, 1).astype(bf16)
        pg1[v * BLOCKS + i] = result
        both = [jnp.concatenate([xg[v * BLOCKS + i, h].astype(f32), p.astype(f32)], axis=0)
                for h, p in enumerate((own_p[i], result))]
        at[i, 0:HALF] = both[0].T.astype(bf16)
        at[i, HALF:] = both[1].T.astype(bf16)
        return carry

    gathers = (pga, pgb, pg1)

    def p_piece(g, vsrc, p):
        rows = BLOCKS // PIECES
        return gathers[g].at[pl.ds(vsrc * BLOCKS + p * rows, rows)]

    def p_ring(g, vsrc, p, sign, hop):
        ref = p_piece(g, vsrc, p)
        push(ref, ref, p_ss.at[g], p_rs.at[g, 0 if sign > 0 else 1, hop - 1, p], at_z(sign))

    def p_first(g, p):
        for sign in (1, -1):
            p_ring(g, v, p, sign, 1)
        ref = p_piece(g, v, p)
        push(ref, ref, pp_ss.at[g], pp_rs.at[g], partner)

    def p_start(g):
        for p in range(PIECES):
            p_first(g, p)

    def p_hop(g, h, pieces=range(PIECES)):
        for p in pieces:
            for sign in (1, -1):
                last = 4 if (p % 2 == 0) == (sign > 0) else 3
                if h > last:
                    continue
                vsrc = ((z - sign * h + NZ) % NZ) * NC + core
                ref = p_piece(g, vsrc, p)
                arrived(ref, p_rs.at[g, 0 if sign > 0 else 1, h - 1, p])
                if h < last:
                    p_ring(g, vsrc, p, sign, h + 1)
                push(ref, ref, pp_ss.at[g], pp_rs.at[g], partner)
        if h == 4 and PIECES - 1 in pieces:
            arrived(gathers[g].at[pl.ds(0, NZ * BLOCKS)], pp_rs.at[g])

    def place(axis, step):
        return (here[axis] + step + 4) % 4

    def right_own(u, i):
        if u == 0:
            return jnp.concatenate([own_p[i], xg[v * BLOCKS + i, 0]], axis=0)
        return jnp.concatenate([pg1[v * BLOCKS + i], xg[v * BLOCKS + i, 1]], axis=0)

    def right_pair(u, i, second):
        base = 2 * u - (7 if second else 3)
        j, k = cand_ref[base, i], cand_ref[base + 1, i]
        pg = pgb if second else pga
        low = low_lanes((SAMP // 2, HALF))
        pj, pk, xj, xk = pg[j], pg[k], xg[j, 0], xg[k, 0]
        top = jnp.where(low, pj.astype(f32), turned(pk))
        bottom = jnp.where(low, turned(pj), pk.astype(f32))
        low = low_lanes((SAMP, HALF))
        if second:
            cols = jnp.where(low, turned(xj), xk.astype(f32))
        else:
            cols = jnp.where(low, xj.astype(f32), turned(xk))
        return jnp.concatenate([top, bottom, cols], axis=0).astype(bf16)

    def right_five(u, i):
        j = cand_ref[5, i]
        pa, pb = pga[j], pgb[j]
        low = low_lanes((SAMP // 2, HALF))
        top = jnp.where(low, pa.astype(f32), turned(pb))
        bottom = jnp.where(low, turned(pa), pb.astype(f32))
        return jnp.concatenate([top.astype(bf16), bottom.astype(bf16), xg[j, 0]], axis=0)

    def right_second(u, i):
        j = cand_ref[u - 6, i]
        return jnp.concatenate([pg1[j], xg[j, 1]], axis=0)

    def stage0(u, right, parts=range(4)):
        slot = u % SLOTS
        for q, d1, d2, s in each():
            if q not in parts:
                continue
            for i4 in range(4):
                i = q * 4 + i4
                term = jnp.dot(at[i], right(u, i), preferred_element_type=f32).astype(bf16)
                for a in range(4):
                    for b in range(4):
                        row = 16 * ((b * NX + a) if d1 == "x" else (a * NX + b))
                        terms[slot, q, a, b, i4] = term[row:row + 16]
            push(terms.at[slot, q, place(d1, 2)], m1.at[u, q], t_ss.at[slot], m1_rs.at[u], at_xy(d1, s))
            push(terms.at[slot, q, place(d1, -s)], m23.at[u, q, 0], t_ss.at[slot], m23_rs.at[u], at_xy(d1, -s))

    def stage1(u):
        slot = u % SLOTS
        arrived(m1.at[u], m1_rs.at[u])
        for q, d1, d2, s in each():
            fwd1[slot, q] = (terms[slot, q, place(d1, s)].astype(f32) + m1[u, q].astype(f32)).astype(bf16)
            push(fwd1.at[slot, q], m23.at[u, q, 1], t_ss.at[slot], m23_rs.at[u], at_xy(d1, s))

    def stage2(u):
        slot = u % SLOTS
        arrived(m23.at[u], m23_rs.at[u])
        for q, d1, d2, s in each():
            part[slot, q] = (terms[slot, q, place(d1, 0)].astype(f32) + m23[u, q, 0].astype(f32)
                             + m23[u, q, 1].astype(f32)).astype(bf16)
            push(part.at[slot, q, place(d2, 2)], n1.at[u, q], r_ss.at[slot], n1_rs.at[u], at_xy(d2, s))
            push(part.at[slot, q, place(d2, -s)], n23.at[u, q, 0], r_ss.at[slot], n23_rs.at[u], at_xy(d2, -s))

    def stage3(u):
        slot = u % SLOTS
        arrived(n1.at[u], n1_rs.at[u])
        for q, d1, d2, s in each():
            fwd2[slot, q] = (part[slot, q, place(d2, s)].astype(f32) + n1[u, q].astype(f32)).astype(bf16)
            push(fwd2.at[slot, q], n23.at[u, q, 1], r_ss.at[slot], n23_rs.at[u], at_xy(d2, s))

    def finish(i, c, qh, total):
        columns = pl.ds(qh * HALF, HALF)
        j = cand_ref[c, i]
        live = count_ref[i]
        slot, found = 0, 0
        for k in range(4):
            match = jnp.where((pat_ref[k, i] == j) & (k < live), 1, 0)
            slot, found = slot + k * match, found + match
        previous = jnp.where(found > 0, wt[i, slot, :, columns], 0.0)
        stepped = previous - step_size * (total * (1.0 / (2.0 * TOTAL)))
        size = jnp.maximum(jnp.abs(stepped) - step_size * penalty, 0.0)
        result = jnp.where(stepped < 0, -size, size)
        if isinstance(c, int) and c == 0:
            rows = l * 16 + lax.broadcasted_iota(jnp.int32, (16, HALF), 0)
            cols = qh * HALF + lax.broadcasted_iota(jnp.int32, (16, HALF), 1)
            on = rows == cols
            diagonal = jnp.where(on, wt[i, 0, :, columns], 1.0)
            result = jnp.where(on, stepped + step_size * (1.0 / diagonal), result)
        out_ref[:, c, i, columns] = result

    def stage4(u, kind):
        slot = u % SLOTS
        arrived(n23.at[u], n23_rs.at[u])
        low = low_lanes((16, HALF))
        for q, d1, d2, s in each():
            for i4 in range(4):
                i = q * 4 + i4
                total = (part[slot, q, place(d2, 0), i4].astype(f32) + n23[u, q, 0, i4].astype(f32)
                         + n23[u, q, 1, i4].astype(f32))
                if kind == "own":
                    finish(i, 0, u, total)
                elif kind == "first":
                    hold[u - 2, i] = total
                elif kind == "pair":
                    before = hold[u - 4, i]
                    finish(i, 2 * u - 7, 0, jnp.where(low, before, turned(total)))
                    finish(i, 2 * u - 6, 0, jnp.where(low, turned(before), total))
                elif kind == "five":
                    finish(i, 5, 0, total)
                else:
                    finish(i, u - 6, 1, total)
        arrived(terms.at[slot, pl.ds(0, 3)], t_ss.at[slot])
        arrived(part.at[slot, pl.ds(0, 3)], r_ss.at[slot])

    lax.fori_loop(0, 4, product_first, 0, unroll=4)
    p_first(0, 0)
    lax.fori_loop(4, 8, product_first, 0, unroll=4)
    p_first(0, 1)
    lax.fori_loop(8, 12, product_first, 0, unroll=4)
    p_first(0, 2)
    lax.fori_loop(12, 16, product_first, 0, unroll=4)
    p_first(0, 3)
    lax.fori_loop(0, 4, product_second, 0, unroll=4)
    lax.fori_loop(4, 8, product_second, 0, unroll=4)
    lax.fori_loop(8, 12, product_second, 0, unroll=4)
    lax.fori_loop(12, 16, product_second, 0, unroll=4)
    stage0(0, right_own)
    p_hop(0, 1)
    stage0(1, right_own)
    p_hop(0, 2, (0, 1))
    stage1(0)
    p_start(1)
    p_hop(0, 2, (2, 3))
    stage1(1)
    p_hop(1, 1)
    p_hop(0, 3)
    stage2(0)
    p_hop(1, 2)
    p_hop(0, 4)
    p_start(2)
    stage2(1)
    p_hop(1, 3)

    def turn(u, carry):
        def when(low, high, what):
            pl.when((u >= low) & (u < high))(what)

        def hops(at, *steps):
            @pl.when(u == at)
            def _():
                for g, h in steps:
                    p_hop(g, h)
                    if (g, h) == (1, 3):
                        p_start(2)

        hops(4, (1, 4))
        hops(7, (2, 4))
        when(2, 4, lambda: stage0(u, lambda u, i: right_pair(u, i, False)))
        when(4, 6, lambda: stage0(u, lambda u, i: right_pair(u, i, True)))
        when(6, 7, lambda: stage0(u, right_five))
        when(7, 12, lambda: stage0(u, right_second))
        a, b, c, d = LAGS
        when(2 + a, 12 + a, lambda: stage1(u - a))
        when(2 + b, 12 + b, lambda: stage2(u - b))
        when(c, 12 + c, lambda: stage3(u - c))
        when(d, d + 1, lambda: stage4(0, "own"))
        when(d + 1, d + 2, lambda: stage4(1, "own"))
        when(d + 2, d + 4, lambda: stage4(u - d, "first"))
        when(d + 4, d + 6, lambda: stage4(u - d, "pair"))
        when(d + 6, d + 7, lambda: stage4(u - d, "five"))
        when(d + 7, d + 12, lambda: stage4(u - d, "second"))
        hops(3, (2, 1))
        hops(4, (2, 2))
        hops(5, (2, 3))
        return carry

    lax.fori_loop(2, CHUNKS + LAGS[3], turn, 0)

    arrived(xg.at[pl.ds(0, 7 * BLOCKS)], x_ss)
    arrived(xg.at[pl.ds(0, 8 * BLOCKS)], xp_ss)
    arrived(wg.at[pl.ds(0, 15)], w_ss)
    for g in range(3):
        arrived(gathers[g].at[pl.ds(0, 7 * BLOCKS)], p_ss.at[g])
        arrived(gathers[g].at[pl.ds(0, 8 * BLOCKS)], pp_ss.at[g])


def body(sample_matrix, precision_blocks, block_pattern, block_counts, candidate_cols):
    vmem = pl.BlockSpec(memory_space=pltpu.VMEM)
    smem = pl.BlockSpec(memory_space=pltpu.SMEM)
    dma = pltpu.SemaphoreType.DMA
    anywhere = pl.BlockSpec(memory_space=pl.ANY)
    scratch = [
        pltpu.VMEM(sample_matrix.shape, bf16),
        pltpu.VMEM(precision_blocks.shape, f32),
        dma((2,)),
        pltpu.VMEM((256, 2, SAMP, HALF), bf16),
        pltpu.VMEM((256, SAMP // 2, HALF), bf16),
        pltpu.VMEM((256, SAMP // 2, HALF), bf16),
        pltpu.VMEM((256, SAMP, HALF), bf16),
        pltpu.VMEM((BLOCKS, SAMP, HALF), bf16),
        pltpu.VMEM((16, 4, 4, 4, 16, 256), bf16),
        pltpu.VMEM((BLOCKS, 4, 16, 256), f32),
        pltpu.VMEM((BLOCKS, 256, 128), bf16),
        pltpu.VMEM((2, BLOCKS, 16, HALF), f32),
        pltpu.VMEM((SLOTS, 4, 4, 4, 4, 16, HALF), bf16),
        pltpu.VMEM((SLOTS, 4, 4, 4, 16, HALF), bf16),
        pltpu.VMEM((SLOTS, 4, 4, 4, 16, HALF), bf16),
        pltpu.VMEM((SLOTS, 4, 4, 16, HALF), bf16),
        pltpu.VMEM((CHUNKS, 4, 4, 4, 16, HALF), bf16),
        pltpu.VMEM((CHUNKS, 4, 2, 4, 4, 16, HALF), bf16),
        pltpu.VMEM((CHUNKS, 4, 4, 16, HALF), bf16),
        pltpu.VMEM((CHUNKS, 4, 2, 4, 16, HALF), bf16),
        dma((2, 4, 4)), dma(()), dma(()), dma(()),
        dma((4, 16)), dma(()),
        dma((3, 2, 4, PIECES)), dma((3,)), dma((3,)), dma((3,)),
        dma((CHUNKS,)), dma((CHUNKS,)), dma((CHUNKS,)), dma((CHUNKS,)), dma((SLOTS,)), dma((SLOTS,)),
    ]
    updated = pl.pallas_call(
        kernel,
        out_shape=jax.ShapeDtypeStruct((16, 6, BLOCKS, 2 * HALF), f32),
        in_specs=[anywhere, anywhere, smem, smem, smem],
        out_specs=vmem,
        scratch_shapes=scratch,
        compiler_params=pltpu.CompilerParams(
            collective_id=0, has_side_effects=True, vmem_limit_bytes=60 * 2 ** 20),
    )(sample_matrix, precision_blocks, block_pattern.T, block_counts, candidate_cols.T)
    return jnp.transpose(updated, (0, 2, 1, 3))


def solution(mesh):
    placed = (
        P("layer", "var"),
        P("layer", "var", None, None),
        P("var", None),
        P("var"),
        P("var", None),
    )
    return jax.shard_map(
        body, mesh=mesh, in_specs=placed, out_specs=P("layer", "var", None, None), check_vma=False
    )
```
